32 devices in a mesh: sec: 16 (over z, x, core), term: 2 (over y).
Axes of the slice: x: 2, y: 2, z: 4, core: 2. Of those that a mesh axis runs over, the one named last changes fastest.
Arguments:
- wavefunction: bfloat16 [64, 128, 2048], P('sec', None, 'term'), may hold values from -6 to 6
- sketch: float32 [64, 128, 32], P('sec'), may hold values from -6 to 6
- kept: int32 [64], P('sec'), may hold values from 8 to 32, as said below
- left_ids: int32 [2048], P(('sec', 'term')), may hold values from 0 to 63, as said below
- right_ids: int32 [2048], P(('sec', 'term')), may hold values from 0 to 63, as said below
- operators: bfloat16 [2048, 128, 128], P(('sec', 'term')), may hold values from -6 to 6
Outputs:
- rotation: bfloat16 [64, 128, 32], P('sec')
- renormalized: float32 [2048, 32, 32], P(('sec', 'term'))
The draws below stay inside these ranges and needn't reach their ends.
Inputs may be any that keep to these rules, and one draw needn't show every extreme that they name: `kept`: at least 8; some sector keeps exactly 32. `left_ids`: block b's left sector is one of the 4 sectors held by sec index b // (64 * 2). `right_ids`: among the 64 blocks of one device (aligned blocks of 64 rows), at most 4 have their right sector among the 4 sectors of any one sec index, and some sec index gets exactly 4 of them.
All inputs are finite; a program needn't handle non-finite values.
Results may differ from the reference program's by a relative error of at most 0.0059.
Values may be sent and summed in bfloat16 or wider, within the bound.
A program may use at most 64 MiB of HBM per device.

```python
import jax
import jax.numpy as jnp
from jax import lax

M = 128
K = 32
SEC_DEV = 4
NB = 64
SECTORS = 64
RIGHT = 2048
BLOCKS = 2048
N_SEC = 16
N_TERM = 2


def draw_kept(key, part):
    values = jax.random.randint(key, (SECTORS,), K // 4, K + 1)
    return values.at[0].set(K).astype(jnp.int32)


def draw_left_ids(key, part):
    index = jnp.arange(BLOCKS, dtype=jnp.int32)
    owner = index // (NB * N_TERM)
    offset = jax.random.randint(key, (BLOCKS,), 0, SEC_DEV)
    return (owner * SEC_DEV + offset).astype(jnp.int32)


def draw_right_ids(key, part):
    groups = BLOCKS // NB
    base = jax.random.fold_in(key, 17)
    keys = jax.random.split(base, groups)
    orders = jax.vmap(lambda sub: jax.random.permutation(sub, N_SEC))(keys)
    position = jnp.arange(NB, dtype=jnp.int32) % N_SEC
    owner = orders[:, position].astype(jnp.int32)
    offset = jax.random.randint(jax.random.fold_in(key, 29), (groups, NB), 0, SEC_DEV)
    return (owner * SEC_DEV + offset).reshape(BLOCKS).astype(jnp.int32)


def level_of(key, dims, shards, least, largest):
    factor_of = 1.0
    for dim, parts in shards:
        heights = jax.random.uniform(jax.random.fold_in(jax.random.fold_in(key, 6), dim), (parts,), jnp.float32, least / len(shards), largest / len(shards))
        factor_of = factor_of * jnp.repeat(jnp.exp(heights), dims[dim] // parts).reshape((-1,) + (1,) * (len(dims) - 1 - dim))
    return factor_of


def centred(rng, dims, scale, bound, cuts=(), held_as=jnp.bfloat16):
    values = scale * jax.random.normal(rng, dims, jnp.float32)
    if cuts:
        values = values * level_of(rng, dims, cuts, -0.22, 0.18)
    return jnp.clip(values, -bound, bound).astype(held_as)


def setup_inputs(seed: int = 0) -> dict:
    key_of = jax.random.split(jax.random.key(seed), 7)
    return {
        "wavefunction": centred(key_of[0], (SECTORS, M, RIGHT), 1.0, 6.0, ((0, 16), (2, 2))),
        "sketch": centred(key_of[1], (SECTORS, M, K), 1.0, 6.0, ((0, 16),), jnp.float32),
        "kept": draw_kept(jax.random.fold_in(key_of[6], 71), 0),
        "left_ids": draw_left_ids(jax.random.fold_in(key_of[6], 71), 0),
        "right_ids": draw_right_ids(jax.random.fold_in(key_of[6], 71), 0),
        "operators": centred(key_of[5], (BLOCKS, M, M), 1.0, 6.0, ((0, 32),)),
    }


HIGH = lax.Precision.HIGHEST

def orthonormal(range_block, lower_block):
    return lax.linalg.triangular_solve(lower_block, range_block, left_side=False, lower=True, transpose_a=True)

def reference(wavefunction, sketch, kept, left_ids, right_ids, operators):
    wave = wavefunction.astype(jnp.float32)
    density = jnp.einsum('smr,snr->smn', wave, wave)
    ranged = jnp.einsum('smn,snk->smk', density, sketch, precision=HIGH)
    gram = jnp.einsum('smk,sml->skl', ranged, ranged, precision=HIGH)
    lower = jnp.linalg.cholesky(gram)
    basis = jax.vmap(orthonormal)(ranged, lower)
    column = jnp.arange(K, dtype=jnp.int32)
    basis = jnp.where(column[None, None, :] < kept[:, None, None], basis, 0.0)
    rotation = basis.astype(jnp.bfloat16)
    groups = BLOCKS // NB

    def one_group(items):
        lefts, rights, ops = items
        left_rot = rotation[lefts].astype(jnp.float32)
        right_rot = rotation[rights].astype(jnp.float32)
        half = jnp.einsum('bmk,bmn->bkn', left_rot, ops.astype(jnp.float32)).astype(jnp.bfloat16)
        return jnp.einsum('bkn,bnl->bkl', half.astype(jnp.float32), right_rot)
    result = lax.map(one_group, (left_ids.reshape(groups, NB), right_ids.reshape(groups, NB), operators.reshape(groups, NB, M, M)))
    return (rotation, result.reshape(BLOCKS, K, K))
```

```python
import functools

import jax
import jax.numpy as jnp
from jax import lax
from jax.experimental import pallas as pl
from jax.experimental.pallas import tpu as pltpu
from jax.sharding import PartitionSpec as P

HIGH = lax.Precision.HIGHEST
MESH = pl.DeviceIdType.MESH
F32 = jnp.float32


def dot_nt(a, b, precision=None):
    return lax.dot_general(
        a, b, (((1,), (1,)), ((), ())), precision=precision, preferred_element_type=F32
    )


def inverse_factors(gram, width):
    row = lax.broadcasted_iota(jnp.int32, gram.shape, 0)
    lane = lax.broadcasted_iota(jnp.int32, gram.shape, 1)
    first = lane // width * width
    eye = jnp.where(lane - first == row, 1.0, 0.0).astype(F32)
    scale = jnp.zeros_like(gram)
    for j in range(width):
        column = jnp.take_along_axis(gram, first + j, axis=1, mode="promise_in_bounds")
        root = lax.rsqrt(column[j : j + 1, :])
        scale = jnp.where(row == j, root, scale)
        if j + 1 < width:
            factor = jnp.where(row > j, column * root, 0.0)
            gram = gram - factor * (gram[j : j + 1, :] * root)
            eye = eye - factor * (eye[j : j + 1, :] * root)
    return eye * scale


def kernel(
    n_sec, n_term, kept_ref, left_ref, right_ref, wave_hbm, sketch_hbm, ops_hbm,
    rot_ref, out_ref,
    wave, sketch, ops, part, rt, every, half,
    wave_sem, sketch_sem, ops_sem, part_send, part_recv, send_sem, recv_sem,
):
    sectors, m, _ = wave.shape
    width = sketch.shape[1]
    blocks = ops.shape[0]
    sec = lax.axis_index("sec")
    term = lax.axis_index("term")
    core = lax.rem(sec, 2)
    side = lax.rem(sec // 2, 2)
    deep = sec // 4
    n_deep = n_sec // 4

    def place(a, b, c):
        return (a * 2 + b) * 2 + c

    terms = [lax.rem(term + t, n_term) for t in range(1, n_term)]
    deeps = [lax.rem(deep + t, n_deep) for t in range(1, n_deep)]
    side_peer = place(deep, 1 - side, core)
    core_peer = place(deep, side, 1 - core)

    waves = []
    for s in range(sectors):
        waves.append(pltpu.make_async_copy(wave_hbm.at[s], wave.at[s], wave_sem.at[s]))
        waves[-1].start()
    get_sketch = pltpu.make_async_copy(sketch_hbm, sketch, sketch_sem)
    get_sketch.start()
    get_ops = pltpu.make_async_copy(ops_hbm, ops, ops_sem)
    get_ops.start()

    barrier = pltpu.get_barrier_semaphore()
    for other in terms:
        pl.semaphore_signal(barrier, inc=1, device_id=(sec, other), device_id_type=MESH)
    peers = [place(a, side, core) for a in deeps] + [side_peer, core_peer]
    for other in peers:
        pl.semaphore_signal(barrier, inc=1, device_id=(other, term), device_id_type=MESH)

    get_sketch.wait()
    part_copies = []
    for s in range(sectors):
        waves[s].wait()
        w = wave[s]
        density = dot_nt(w, w)
        part[term, s] = jnp.dot(sketch[s], density, precision=HIGH, preferred_element_type=F32)
        if s == 0:
            pl.semaphore_wait(barrier, len(terms) + len(peers))
        for t, other in enumerate(terms):
            copy = pltpu.make_async_remote_copy(
                src_ref=part.at[term, s],
                dst_ref=part.at[term, s],
                send_sem=part_send.at[t, s],
                recv_sem=part_recv.at[term, s],
                device_id=(sec, other),
                device_id_type=MESH,
            )
            copy.start()
            part_copies.append(copy)
    for s in range(sectors):
        for other in terms:
            pltpu.make_async_remote_copy(
                src_ref=part.at[other, s],
                dst_ref=part.at[other, s],
                send_sem=part_send.at[0, s],
                recv_sem=part_recv.at[other, s],
                device_id=(sec, other),
                device_id_type=MESH,
            ).wait_recv()
    total = part[0]
    for t in range(1, n_term):
        total = total + part[t]
    total = total.reshape(sectors * width, m)

    full = dot_nt(total, total, HIGH)
    owner = lax.broadcasted_iota(jnp.int32, (width, sectors * width), 1) // width
    gram = full[:width]
    for s in range(1, sectors):
        gram = jnp.where(owner == s, full[s * width : (s + 1) * width], gram)
    inverse = inverse_factors(gram, width)
    spread = jnp.concatenate([jnp.where(owner == s, inverse, 0.0) for s in range(sectors)], axis=0)
    basis = jnp.dot(spread, total, precision=HIGH, preferred_element_type=F32)
    basis = basis.reshape(sectors, width, m)
    row = lax.broadcasted_iota(jnp.int32, (width, m), 0)
    for s in range(sectors):
        kept_rows = jnp.where(row < kept_ref[s], basis[s], 0.0).astype(jnp.bfloat16)
        rt[s] = kept_rows
        every[sec * sectors + s] = kept_rows

    sends = []

    def send(src, slot, device):
        copy = pltpu.make_async_remote_copy(
            src_ref=src,
            dst_ref=every.at[pl.ds(slot * sectors, sectors)],
            send_sem=send_sem.at[len(sends)],
            recv_sem=recv_sem.at[slot],
            device_id=(device, term),
            device_id_type=MESH,
        )
        copy.start()
        sends.append(copy)

    def arrived(slot):
        part_of = every.at[pl.ds(slot * sectors, sectors)]
        pltpu.make_async_remote_copy(
            src_ref=part_of,
            dst_ref=part_of,
            send_sem=send_sem.at[0],
            recv_sem=recv_sem.at[slot],
            device_id=(core_peer, term),
            device_id_type=MESH,
        ).wait_recv()
        return part_of

    for a in deeps:
        send(rt, sec, place(a, side, core))
    send(rt, sec, side_peer)
    send(rt, sec, core_peer)

    get_ops.wait()

    def left_side(start, stop):
        @pl.loop(start, stop, step=8)
        def _(first):
            for i in range(8):
                b = first + i
                rotated = jnp.dot(rt[lax.rem(left_ref[b], sectors)], ops[b], preferred_element_type=F32)
                half[b] = rotated.astype(jnp.bfloat16)

    left_side(0, blocks // 2)
    for a in deeps:
        slot = place(a, side, core)
        block = arrived(slot)
        send(block, slot, side_peer)
        send(block, slot, core_peer)
    left_side(blocks // 2, blocks)
    for a in [deep] + deeps:
        slot = place(a, 1 - side, core)
        block = arrived(slot)
        send(block, slot, core_peer)
    for s in range(sectors):
        rot_ref[s] = rt[s]
    for a in [deep] + deeps:
        for b in range(2):
            arrived(place(a, b, 1 - core))

    @pl.loop(0, blocks, step=8)
    def _(first):
        for i in range(8):
            b = first + i
            out_ref[b] = dot_nt(half[b], every[right_ref[b]])

    for copy in part_copies + sends:
        copy.wait_send()


def shards(n_sec, n_term, wavefunction, sketch, kept, left_ids, right_ids, operators):
    sectors, m, right = wavefunction.shape
    width = sketch.shape[2]
    blocks = operators.shape[0]
    n_deep = n_sec // 4
    n_sends = (n_deep - 1) + 2 + 2 * (n_deep - 1) + n_deep
    smem = pl.BlockSpec(memory_space=pltpu.SMEM)
    hbm = pl.BlockSpec(memory_space=pl.ANY)
    vmem = pl.BlockSpec(memory_space=pltpu.VMEM)
    dma = pltpu.SemaphoreType.DMA
    rotation, result = pl.pallas_call(
        functools.partial(kernel, n_sec, n_term),
        out_shape=(
            jax.ShapeDtypeStruct((sectors, width, m), jnp.bfloat16),
            jax.ShapeDtypeStruct((blocks, width, width), F32),
        ),
        in_specs=[smem, smem, smem, hbm, hbm, hbm],
        out_specs=(vmem, vmem),
        scratch_shapes=[
            pltpu.VMEM((sectors, m, right), jnp.bfloat16),
            pltpu.VMEM((sectors, width, m), F32),
            pltpu.VMEM((blocks, m, m), jnp.bfloat16),
            pltpu.VMEM((n_term, sectors, width, m), F32),
            pltpu.VMEM((sectors, width, m), jnp.bfloat16),
            pltpu.VMEM((n_sec * sectors, width, m), jnp.bfloat16),
            pltpu.VMEM((blocks, width, m), jnp.bfloat16),
            dma((sectors,)),
            dma,
            dma,
            dma((max(n_term - 1, 1), sectors)),
            dma((n_term, sectors)),
            dma((n_sends,)),
            dma((n_sec,)),
        ],
        compiler_params=pltpu.CompilerParams(
            collective_id=0, has_side_effects=True, vmem_limit_bytes=32 * 1024 * 1024
        ),
    )(kept, left_ids, right_ids, wavefunction, jnp.swapaxes(sketch, 1, 2), operators)
    return jnp.swapaxes(rotation, 1, 2), result


def solution(mesh):
    in_specs = (
        P("sec", None, "term"),
        P("sec", None, None),
        P("sec"),
        P(("sec", "term")),
        P(("sec", "term")),
        P(("sec", "term"), None, None),
    )
    out_specs = (P("sec", None, None), P(("sec", "term"), None, None))
    run = functools.partial(shards, mesh.shape["sec"], mesh.shape["term"])
    return jax.shard_map(run, mesh=mesh, in_specs=in_specs, out_specs=out_specs, check_vma=False)
```

```python
import functools

import jax
import jax.numpy as jnp
from jax import lax
from jax.experimental import pallas as pl
from jax.experimental.pallas import tpu as pltpu
from jax.sharding import PartitionSpec as P

HIGH = lax.Precision.HIGHEST
MESH = pl.DeviceIdType.MESH
F32 = jnp.float32


def dot_nt(a, b, precision=None):
    return lax.dot_general(
        a, b, (((1,), (1,)), ((), ())), precision=precision, preferred_element_type=F32
    )


def inverse_factors(gram, width):
    row = lax.broadcasted_iota(jnp.int32, gram.shape, 0)
    lane = lax.broadcasted_iota(jnp.int32, gram.shape, 1)
    first = lane // width * width
    eye = jnp.where(lane - first == row, 1.0, 0.0).astype(F32)
    scale = jnp.zeros_like(gram)
    for j in range(width):
        column = jnp.take_along_axis(gram, first + j, axis=1, mode="promise_in_bounds")
        root = lax.rsqrt(column[j : j + 1, :])
        scale = jnp.where(row == j, root, scale)
        if j + 1 < width:
            factor = jnp.where(row > j, column * root, 0.0)
            gram = gram - factor * (gram[j : j + 1, :] * root)
            eye = eye - factor * (eye[j : j + 1, :] * root)
    return eye * scale


def kernel(
    n_sec, n_term, kept_hbm, left_hbm, right_hbm, wave_hbm, sketch_hbm, ops_hbm,
    rot_ref, out_ref,
    kept_ref, left_ref, right_ref, ids_sem, wave, sketch, ops, part, rt, every, half,
    wave_sem, sketch_sem, ops_sem, part_send, part_recv, send_sem, recv_sem,
):
    sectors, m, _ = wave.shape
    width = sketch.shape[1]
    blocks = ops.shape[0]
    sec = lax.axis_index("sec")
    term = lax.axis_index("term")
    core = lax.rem(sec, 2)
    side = lax.rem(sec // 2, 2)
    deep = sec // 4
    n_deep = n_sec // 4

    def place(a, b, c):
        return (a * 2 + b) * 2 + c

    terms = [lax.rem(term + t, n_term) for t in range(1, n_term)]
    deeps = [lax.rem(deep + t, n_deep) for t in range(1, n_deep)]
    side_peer = place(deep, 1 - side, core)
    core_peer = place(deep, side, 1 - core)

    waves = []
    for s in range(sectors):
        waves.append(pltpu.make_async_copy(wave_hbm.at[s], wave.at[s], wave_sem.at[s]))
        waves[-1].start()
    get_sketch = pltpu.make_async_copy(sketch_hbm, sketch, sketch_sem)
    get_sketch.start()
    get_ops = pltpu.make_async_copy(ops_hbm, ops, ops_sem)
    get_ops.start()
    get_ids = []
    for i, (src, dst) in enumerate(((kept_hbm, kept_ref), (left_hbm, left_ref), (right_hbm, right_ref))):
        get_ids.append(pltpu.make_async_copy(src, dst, ids_sem.at[i]))
        get_ids[-1].start()

    barrier = pltpu.get_barrier_semaphore()
    for other in terms:
        pl.semaphore_signal(barrier, inc=1, device_id=(sec, other), device_id_type=MESH)
    peers = [place(a, side, core) for a in deeps] + [side_peer, core_peer]
    for other in peers:
        pl.semaphore_signal(barrier, inc=1, device_id=(other, term), device_id_type=MESH)

    get_sketch.wait()
    part_copies = []
    for s in range(sectors):
        waves[s].wait()
        w = wave[s]
        density = dot_nt(w, w)
        part[term, s] = jnp.dot(sketch[s], density, precision=HIGH, preferred_element_type=F32)
        if s == 0:
            pl.semaphore_wait(barrier, len(terms) + len(peers))
        for t, other in enumerate(terms):
            copy = pltpu.make_async_remote_copy(
                src_ref=part.at[term, s],
                dst_ref=part.at[term, s],
                send_sem=part_send.at[t, s],
                recv_sem=part_recv.at[term, s],
                device_id=(sec, other),
                device_id_type=MESH,
            )
            copy.start()
            part_copies.append(copy)
    for s in range(sectors):
        for other in terms:
            pltpu.make_async_remote_copy(
                src_ref=part.at[other, s],
                dst_ref=part.at[other, s],
                send_sem=part_send.at[0, s],
                recv_sem=part_recv.at[other, s],
                device_id=(sec, other),
                device_id_type=MESH,
            ).wait_recv()
    for copy in get_ids:
        copy.wait()
    total = part[0]
    for t in range(1, n_term):
        total = total + part[t]
    total = total.reshape(sectors * width, m)

    full = dot_nt(total, total, HIGH)
    owner = lax.broadcasted_iota(jnp.int32, (width, sectors * width), 1) // width
    gram = full[:width]
    for s in range(1, sectors):
        gram = jnp.where(owner == s, full[s * width : (s + 1) * width], gram)
    inverse = inverse_factors(gram, width)
    spread = jnp.concatenate([jnp.where(owner == s, inverse, 0.0) for s in range(sectors)], axis=0)
    basis = jnp.dot(spread, total, precision=HIGH, preferred_element_type=F32)
    basis = basis.reshape(sectors, width, m)
    row = lax.broadcasted_iota(jnp.int32, (width, m), 0)
    for s in range(sectors):
        kept_rows = jnp.where(row < kept_ref[s], basis[s], 0.0).astype(jnp.bfloat16)
        rt[s] = kept_rows
        every[sec * sectors + s] = kept_rows

    sends = []

    def send(src, slot, device):
        copy = pltpu.make_async_remote_copy(
            src_ref=src,
            dst_ref=every.at[pl.ds(slot * sectors, sectors)],
            send_sem=send_sem.at[len(sends)],
            recv_sem=recv_sem.at[slot],
            device_id=(device, term),
            device_id_type=MESH,
        )
        copy.start()
        sends.append(copy)

    def arrived(slot):
        part_of = every.at[pl.ds(slot * sectors, sectors)]
        pltpu.make_async_remote_copy(
            src_ref=part_of,
            dst_ref=part_of,
            send_sem=send_sem.at[0],
            recv_sem=recv_sem.at[slot],
            device_id=(core_peer, term),
            device_id_type=MESH,
        ).wait_recv()
        return part_of

    for a in deeps:
        send(rt, sec, place(a, side, core))
    send(rt, sec, side_peer)
    send(rt, sec, core_peer)

    get_ops.wait()

    def left_side(start, stop):
        @pl.loop(start, stop, step=8)
        def _(first):
            for i in range(8):
                b = first + i
                rotated = jnp.dot(rt[lax.rem(left_ref[b], sectors)], ops[b], preferred_element_type=F32)
                half[b] = rotated.astype(jnp.bfloat16)

    left_side(0, blocks // 2)
    for a in deeps:
        slot = place(a, side, core)
        block = arrived(slot)
        send(block, slot, side_peer)
        send(block, slot, core_peer)
    left_side(blocks // 2, blocks)
    for a in [deep] + deeps:
        slot = place(a, 1 - side, core)
        block = arrived(slot)
        send(block, slot, core_peer)
    for s in range(sectors):
        rot_ref[s] = rt[s]
    for a in [deep] + deeps:
        for b in range(2):
            arrived(place(a, b, 1 - core))

    @pl.loop(0, blocks, step=8)
    def _(first):
        for i in range(8):
            b = first + i
            out_ref[b] = dot_nt(half[b], every[right_ref[b]])

    for copy in part_copies + sends:
        copy.wait_send()


def shards(n_sec, n_term, wavefunction, sketch, kept, left_ids, right_ids, operators):
    sectors, m, right = wavefunction.shape
    width = sketch.shape[2]
    blocks = operators.shape[0]
    n_deep = n_sec // 4
    n_sends = (n_deep - 1) + 2 + 2 * (n_deep - 1) + n_deep
    hbm = pl.BlockSpec(memory_space=pl.ANY)
    vmem = pl.BlockSpec(memory_space=pltpu.VMEM)
    dma = pltpu.SemaphoreType.DMA
    rotation, result = pl.pallas_call(
        functools.partial(kernel, n_sec, n_term),
        out_shape=(
            jax.ShapeDtypeStruct((sectors, width, m), jnp.bfloat16),
            jax.ShapeDtypeStruct((blocks, width, width), F32),
        ),
        in_specs=[hbm] * 6,
        out_specs=(vmem, vmem),
        scratch_shapes=[
            pltpu.SMEM((sectors,), jnp.int32),
            pltpu.SMEM((blocks,), jnp.int32),
            pltpu.SMEM((blocks,), jnp.int32),
            pltpu.SemaphoreType.DMA((3,)),
            pltpu.VMEM((sectors, m, right), jnp.bfloat16),
            pltpu.VMEM((sectors, width, m), F32),
            pltpu.VMEM((blocks, m, m), jnp.bfloat16),
            pltpu.VMEM((n_term, sectors, width, m), F32),
            pltpu.VMEM((sectors, width, m), jnp.bfloat16),
            pltpu.VMEM((n_sec * sectors, width, m), jnp.bfloat16),
            pltpu.VMEM((blocks, width, m), jnp.bfloat16),
            dma((sectors,)),
            dma,
            dma,
            dma((max(n_term - 1, 1), sectors)),
            dma((n_term, sectors)),
            dma((n_sends,)),
            dma((n_sec,)),
        ],
        compiler_params=pltpu.CompilerParams(
            collective_id=0, has_side_effects=True, vmem_limit_bytes=62 * 1024 * 1024
        ),
    )(kept, left_ids, right_ids, wavefunction, jnp.swapaxes(sketch, 1, 2), operators)
    return jnp.swapaxes(rotation, 1, 2), result


def solution(mesh):
    in_specs = (
        P("sec", None, "term"),
        P("sec", None, None),
        P("sec"),
        P(("sec", "term")),
        P(("sec", "term")),
        P(("sec", "term"), None, None),
    )
    out_specs = (P("sec", None, None), P(("sec", "term"), None, None))
    run = functools.partial(shards, mesh.shape["sec"], mesh.shape["term"])
    return jax.shard_map(run, mesh=mesh, in_specs=in_specs, out_specs=out_specs, check_vma=False)
```

```python
import functools

import jax
import jax.numpy as jnp
from jax import lax
from jax.experimental import pallas as pl
from jax.experimental.pallas import tpu as pltpu
from jax.sharding import PartitionSpec as P

HIGH = lax.Precision.HIGHEST
MESH = pl.DeviceIdType.MESH
F32 = jnp.float32


def dot_nt(a, b, precision=None):
    return lax.dot_general(
        a, b, (((1,), (1,)), ((), ())), precision=precision, preferred_element_type=F32
    )


def inverse_factors(gram, width):
    row = lax.broadcasted_iota(jnp.int32, gram.shape, 0)
    lane = lax.broadcasted_iota(jnp.int32, gram.shape, 1)
    first = lane // width * width
    eye = jnp.where(lane - first == row, 1.0, 0.0).astype(F32)
    scale = jnp.zeros_like(gram)
    for j in range(width):
        column = jnp.take_along_axis(gram, first + j, axis=1, mode="promise_in_bounds")
        root = lax.rsqrt(column[j : j + 1, :])
        scale = jnp.where(row == j, root, scale)
        if j + 1 < width:
            factor = jnp.where(row > j, column * root, 0.0)
            gram = gram - factor * (gram[j : j + 1, :] * root)
            eye = eye - factor * (eye[j : j + 1, :] * root)
    return eye * scale


def kernel(
    n_sec, n_term, kept_hbm, left_hbm, wave_hbm, sketch_hbm, ops_hbm,
    rot_out, half_out, every_out,
    kept_ref, left_ref, ids_sem, out_sem, wave, sketch, ops, part, rt, every, half,
    wave_sem, sketch_sem, ops_sem, part_send, part_recv, send_sem, recv_sem,
):
    sectors, m, _ = wave.shape
    width = sketch.shape[1]
    blocks = ops.shape[0]
    sec = lax.axis_index("sec")
    term = lax.axis_index("term")
    core = lax.rem(sec, 2)
    side = lax.rem(sec // 2, 2)
    deep = sec // 4
    n_deep = n_sec // 4

    def place(a, b, c):
        return (a * 2 + b) * 2 + c

    terms = [lax.rem(term + t, n_term) for t in range(1, n_term)]
    deeps = [lax.rem(deep + t, n_deep) for t in range(1, n_deep)]
    side_peer = place(deep, 1 - side, core)
    core_peer = place(deep, side, 1 - core)

    waves = []
    for s in range(sectors):
        waves.append(pltpu.make_async_copy(wave_hbm.at[s], wave.at[s], wave_sem.at[s]))
        waves[-1].start()
    get_sketch = pltpu.make_async_copy(sketch_hbm, sketch, sketch_sem)
    get_sketch.start()
    get_ops = pltpu.make_async_copy(ops_hbm, ops, ops_sem)
    get_ops.start()
    get_ids = []
    for i, (src, dst) in enumerate(((kept_hbm, kept_ref), (left_hbm, left_ref))):
        get_ids.append(pltpu.make_async_copy(src, dst, ids_sem.at[i]))
        get_ids[-1].start()

    barrier = pltpu.get_barrier_semaphore()
    for other in terms:
        pl.semaphore_signal(barrier, inc=1, device_id=(sec, other), device_id_type=MESH)
    peers = [place(a, side, core) for a in deeps] + [side_peer, core_peer]
    for other in peers:
        pl.semaphore_signal(barrier, inc=1, device_id=(other, term), device_id_type=MESH)

    get_sketch.wait()
    part_copies = []
    for s in range(sectors):
        waves[s].wait()
        w = wave[s]
        density = dot_nt(w, w)
        part[term, s] = jnp.dot(sketch[s], density, precision=HIGH, preferred_element_type=F32)
        if s == 0:
            pl.semaphore_wait(barrier, len(terms) + len(peers))
        for t, other in enumerate(terms):
            copy = pltpu.make_async_remote_copy(
                src_ref=part.at[term, s],
                dst_ref=part.at[term, s],
                send_sem=part_send.at[t, s],
                recv_sem=part_recv.at[term, s],
                device_id=(sec, other),
                device_id_type=MESH,
            )
            copy.start()
            part_copies.append(copy)
    for s in range(sectors):
        for other in terms:
            pltpu.make_async_remote_copy(
                src_ref=part.at[other, s],
                dst_ref=part.at[other, s],
                send_sem=part_send.at[0, s],
                recv_sem=part_recv.at[other, s],
                device_id=(sec, other),
                device_id_type=MESH,
            ).wait_recv()
    for copy in get_ids:
        copy.wait()
    total = part[0]
    for t in range(1, n_term):
        total = total + part[t]
    total = total.reshape(sectors * width, m)

    full = dot_nt(total, total, HIGH)
    owner = lax.broadcasted_iota(jnp.int32, (width, sectors * width), 1) // width
    gram = full[:width]
    for s in range(1, sectors):
        gram = jnp.where(owner == s, full[s * width : (s + 1) * width], gram)
    inverse = inverse_factors(gram, width)
    spread = jnp.concatenate([jnp.where(owner == s, inverse, 0.0) for s in range(sectors)], axis=0)
    basis = jnp.dot(spread, total, precision=HIGH, preferred_element_type=F32)
    basis = basis.reshape(sectors, width, m)
    row = lax.broadcasted_iota(jnp.int32, (width, m), 0)
    for s in range(sectors):
        kept_rows = jnp.where(row < kept_ref[s], basis[s], 0.0).astype(jnp.bfloat16)
        rt[s] = kept_rows
        every[sec * sectors + s] = kept_rows

    sends = []

    def send(src, slot, device):
        copy = pltpu.make_async_remote_copy(
            src_ref=src,
            dst_ref=every.at[pl.ds(slot * sectors, sectors)],
            send_sem=send_sem.at[len(sends)],
            recv_sem=recv_sem.at[slot],
            device_id=(device, term),
            device_id_type=MESH,
        )
        copy.start()
        sends.append(copy)

    def arrived(slot):
        part_of = every.at[pl.ds(slot * sectors, sectors)]
        pltpu.make_async_remote_copy(
            src_ref=part_of,
            dst_ref=part_of,
            send_sem=send_sem.at[0],
            recv_sem=recv_sem.at[slot],
            device_id=(core_peer, term),
            device_id_type=MESH,
        ).wait_recv()
        return part_of

    for a in deeps:
        send(rt, sec, place(a, side, core))
    send(rt, sec, side_peer)
    send(rt, sec, core_peer)

    outs = [pltpu.make_async_copy(rt, rot_out, out_sem.at[0])]
    outs[0].start()
    get_ops.wait()

    def left_side(start, stop):
        @pl.loop(start, stop, step=8)
        def _(first):
            for i in range(8):
                b = first + i
                rotated = jnp.dot(rt[lax.rem(left_ref[b], sectors)], ops[b], preferred_element_type=F32)
                half[b] = rotated.astype(jnp.bfloat16)

    left_side(0, blocks // 2)
    for a in deeps:
        slot = place(a, side, core)
        block = arrived(slot)
        send(block, slot, side_peer)
        send(block, slot, core_peer)
    left_side(blocks // 2, blocks)
    outs.append(pltpu.make_async_copy(half, half_out, out_sem.at[1]))
    outs[1].start()
    for a in [deep] + deeps:
        slot = place(a, 1 - side, core)
        block = arrived(slot)
        send(block, slot, core_peer)
    for a in [deep] + deeps:
        for b in range(2):
            arrived(place(a, b, 1 - core))

    outs.append(pltpu.make_async_copy(every, every_out, out_sem.at[2]))
    outs[2].start()
    for copy in outs:
        copy.wait()
    for copy in part_copies + sends:
        copy.wait_send()


def right_kernel(right_ref, rot_in, half, every, rot_out, out_ref, result):
    blocks, width, _ = half.shape
    rot_out[...] = rot_in[...]

    @pl.loop(0, blocks, step=8)
    def _(first):
        for i in range(8):
            b = first + i
            rows = pl.ds(pl.multiple_of(b * width, width), width)
            result[rows, :width] = dot_nt(half[b], every[right_ref[b]])

    for k in range(width):
        out_ref[k] = result[pl.ds(k, blocks, stride=width), :][:, :width].T


def shards(n_sec, n_term, wavefunction, sketch, kept, left_ids, right_ids, operators):
    sectors, m, right = wavefunction.shape
    width = sketch.shape[2]
    blocks = operators.shape[0]
    n_deep = n_sec // 4
    n_sends = (n_deep - 1) + 2 + 2 * (n_deep - 1) + n_deep
    hbm = pl.BlockSpec(memory_space=pl.ANY)
    vmem = pl.BlockSpec(memory_space=pltpu.VMEM)
    dma = pltpu.SemaphoreType.DMA
    rotation, half, every = pl.pallas_call(
        functools.partial(kernel, n_sec, n_term),
        out_shape=(
            jax.ShapeDtypeStruct((sectors, width, m), jnp.bfloat16),
            jax.ShapeDtypeStruct((blocks, width, m), jnp.bfloat16),
            jax.ShapeDtypeStruct((n_sec * sectors, width, m), jnp.bfloat16),
        ),
        in_specs=[hbm] * 5,
        out_specs=(hbm, hbm, hbm),
        scratch_shapes=[
            pltpu.SMEM((sectors,), jnp.int32),
            pltpu.SMEM((blocks,), jnp.int32),
            pltpu.SemaphoreType.DMA((2,)),
            pltpu.SemaphoreType.DMA((3,)),
            pltpu.VMEM((sectors, m, right), jnp.bfloat16),
            pltpu.VMEM((sectors, width, m), F32),
            pltpu.VMEM((blocks, m, m), jnp.bfloat16),
            pltpu.VMEM((n_term, sectors, width, m), F32),
            pltpu.VMEM((sectors, width, m), jnp.bfloat16),
            pltpu.VMEM((n_sec * sectors, width, m), jnp.bfloat16),
            pltpu.VMEM((blocks, width, m), jnp.bfloat16),
            dma((sectors,)),
            dma,
            dma,
            dma((max(n_term - 1, 1), sectors)),
            dma((n_term, sectors)),
            dma((n_sends,)),
            dma((n_sec,)),
        ],
        compiler_params=pltpu.CompilerParams(
            collective_id=0, has_side_effects=True, vmem_limit_bytes=62 * 1024 * 1024
        ),
    )(kept, left_ids, wavefunction, jnp.swapaxes(sketch, 1, 2), operators)
    rotation, result = pl.pallas_call(
        right_kernel,
        out_shape=(
            jax.ShapeDtypeStruct((sectors, width, m), jnp.bfloat16),
            jax.ShapeDtypeStruct((width, width, blocks), F32),
        ),
        in_specs=[pl.BlockSpec(memory_space=pltpu.SMEM), vmem, vmem, vmem],
        out_specs=(vmem, vmem),
        scratch_shapes=[pltpu.VMEM((blocks * width, 128), F32)],
        compiler_params=pltpu.CompilerParams(vmem_limit_bytes=62 * 1024 * 1024),
    )(right_ids, rotation, half, every)
    return jnp.swapaxes(rotation, 1, 2), jnp.transpose(result, (2, 0, 1))


def solution(mesh):
    in_specs = (
        P("sec", None, "term"),
        P("sec", None, None),
        P("sec"),
        P(("sec", "term")),
        P(("sec", "term")),
        P(("sec", "term"), None, None),
    )
    out_specs = (P("sec", None, None), P(("sec", "term"), None, None))
    run = functools.partial(shards, mesh.shape["sec"], mesh.shape["term"])
    return jax.shard_map(run, mesh=mesh, in_specs=in_specs, out_specs=out_specs, check_vma=False)
```

```python
import functools

import jax
import jax.numpy as jnp
from jax import lax
from jax.experimental import pallas as pl
from jax.experimental.pallas import tpu as pltpu
from jax.sharding import PartitionSpec as P

HIGH = lax.Precision.HIGHEST
MESH = pl.DeviceIdType.MESH
F32 = jnp.float32


def dot_nt(a, b, precision=None):
    return lax.dot_general(
        a, b, (((1,), (1,)), ((), ())), precision=precision, preferred_element_type=F32
    )


def inverse_factors(gram, width):
    row = lax.broadcasted_iota(jnp.int32, gram.shape, 0)
    lane = lax.broadcasted_iota(jnp.int32, gram.shape, 1)
    first = lane // width * width
    eye = jnp.where(lane - first == row, 1.0, 0.0).astype(F32)
    scale = jnp.zeros_like(gram)
    for j in range(width):
        column = jnp.take_along_axis(gram, first + j, axis=1, mode="promise_in_bounds")
        root = lax.rsqrt(column[j : j + 1, :])
        scale = jnp.where(row == j, root, scale)
        if j + 1 < width:
            factor = jnp.where(row > j, column * root, 0.0)
            gram = gram - factor * (gram[j : j + 1, :] * root)
            eye = eye - factor * (eye[j : j + 1, :] * root)
    return eye * scale


def kernel(
    n_sec, n_term, kept_hbm, left_hbm, wave_hbm, sketch_hbm, ops_hbm,
    rot_out, half_out, every_out,
    kept_ref, left_ref, ids_sem, out_sem, wave, sketch, ops, part, rt, every, half,
    wave_sem, sketch_sem, ops_sem, part_send, part_recv, send_sem, recv_sem,
):
    sectors, m, _ = wave.shape
    width = sketch.shape[1]
    blocks = ops.shape[0]
    sec = lax.axis_index("sec")
    term = lax.axis_index("term")
    core = lax.rem(sec, 2)
    side = lax.rem(sec // 2, 2)
    deep = sec // 4
    n_deep = n_sec // 4

    def place(a, b, c):
        return (a * 2 + b) * 2 + c

    terms = [lax.rem(term + t, n_term) for t in range(1, n_term)]
    deeps = [lax.rem(deep + t, n_deep) for t in range(1, n_deep)]
    side_peer = place(deep, 1 - side, core)
    core_peer = place(deep, side, 1 - core)

    waves = []
    for s in range(sectors):
        waves.append(pltpu.make_async_copy(wave_hbm.at[s], wave.at[s], wave_sem.at[s]))
        waves[-1].start()
    get_sketch = pltpu.make_async_copy(sketch_hbm, sketch, sketch_sem)
    get_sketch.start()
    get_ops = pltpu.make_async_copy(ops_hbm, ops, ops_sem)
    get_ops.start()
    get_ids = []
    for i, (src, dst) in enumerate(((kept_hbm, kept_ref), (left_hbm, left_ref))):
        get_ids.append(pltpu.make_async_copy(src, dst, ids_sem.at[i]))
        get_ids[-1].start()

    barrier = pltpu.get_barrier_semaphore()
    for other in terms:
        pl.semaphore_signal(barrier, inc=1, device_id=(sec, other), device_id_type=MESH)
    peers = [place(a, side, core) for a in deeps] + [side_peer, core_peer]
    for other in peers:
        pl.semaphore_signal(barrier, inc=1, device_id=(other, term), device_id_type=MESH)

    get_sketch.wait()
    part_copies = []
    for s in range(sectors):
        waves[s].wait()
        w = wave[s]
        density = dot_nt(w, w)
        part[term, s] = jnp.dot(sketch[s], density, precision=HIGH, preferred_element_type=F32)
        if s == 0:
            pl.semaphore_wait(barrier, len(terms) + len(peers))
        for t, other in enumerate(terms):
            copy = pltpu.make_async_remote_copy(
                src_ref=part.at[term, s],
                dst_ref=part.at[term, s],
                send_sem=part_send.at[t, s],
                recv_sem=part_recv.at[term, s],
                device_id=(sec, other),
                device_id_type=MESH,
            )
            copy.start()
            part_copies.append(copy)
    for s in range(sectors):
        for other in terms:
            pltpu.make_async_remote_copy(
                src_ref=part.at[other, s],
                dst_ref=part.at[other, s],
                send_sem=part_send.at[0, s],
                recv_sem=part_recv.at[other, s],
                device_id=(sec, other),
                device_id_type=MESH,
            ).wait_recv()
    for copy in get_ids:
        copy.wait()
    total = part[0]
    for t in range(1, n_term):
        total = total + part[t]
    total = total.reshape(sectors * width, m)

    full = dot_nt(total, total, HIGH)
    owner = lax.broadcasted_iota(jnp.int32, (width, sectors * width), 1) // width
    gram = full[:width]
    for s in range(1, sectors):
        gram = jnp.where(owner == s, full[s * width : (s + 1) * width], gram)
    inverse = inverse_factors(gram, width)
    spread = jnp.concatenate([jnp.where(owner == s, inverse, 0.0) for s in range(sectors)], axis=0)
    basis = jnp.dot(spread, total, precision=HIGH, preferred_element_type=F32)
    basis = basis.reshape(sectors, width, m)
    row = lax.broadcasted_iota(jnp.int32, (width, m), 0)
    for s in range(sectors):
        kept_rows = jnp.where(row < kept_ref[s], basis[s], 0.0).astype(jnp.bfloat16)
        rt[s] = kept_rows
        every[sec * sectors + s] = kept_rows

    sends = []

    def send(src, slot, device):
        copy = pltpu.make_async_remote_copy(
            src_ref=src,
            dst_ref=every.at[pl.ds(slot * sectors, sectors)],
            send_sem=send_sem.at[len(sends)],
            recv_sem=recv_sem.at[slot],
            device_id=(device, term),
            device_id_type=MESH,
        )
        copy.start()
        sends.append(copy)

    def keep(slot):
        rows = pl.ds(slot * sectors, sectors)
        outs.append(pltpu.make_async_copy(every.at[rows], every_out.at[rows], out_sem.at[len(outs)]))
        outs[-1].start()

    def arrived(slot):
        part_of = every.at[pl.ds(slot * sectors, sectors)]
        pltpu.make_async_remote_copy(
            src_ref=part_of,
            dst_ref=part_of,
            send_sem=send_sem.at[0],
            recv_sem=recv_sem.at[slot],
            device_id=(core_peer, term),
            device_id_type=MESH,
        ).wait_recv()
        keep(slot)
        return part_of

    for a in deeps:
        send(rt, sec, place(a, side, core))
    send(rt, sec, side_peer)
    send(rt, sec, core_peer)

    outs = [pltpu.make_async_copy(rt, rot_out, out_sem.at[0])]
    outs[0].start()
    keep(sec)
    get_ops.wait()

    def left_side(start, stop):
        @pl.loop(start, stop, step=8)
        def _(first):
            for i in range(8):
                b = first + i
                rotated = jnp.dot(rt[lax.rem(left_ref[b], sectors)], ops[b], preferred_element_type=F32)
                half[b] = rotated.astype(jnp.bfloat16)

    left_side(0, blocks // 2)
    for a in deeps:
        slot = place(a, side, core)
        block = arrived(slot)
        send(block, slot, side_peer)
        send(block, slot, core_peer)
    left_side(blocks // 2, blocks)
    outs.append(pltpu.make_async_copy(half, half_out, out_sem.at[len(outs)]))
    outs[-1].start()
    for a in [deep] + deeps:
        slot = place(a, 1 - side, core)
        block = arrived(slot)
        send(block, slot, core_peer)
    for a in [deep] + deeps:
        for b in range(2):
            arrived(place(a, b, 1 - core))

    for copy in outs:
        copy.wait()
    for copy in part_copies + sends:
        copy.wait_send()


def right_kernel(
    right_hbm, rot_in, half_hbm, every_hbm, rot_out, out_hbm,
    right_ref, half, every, result, flipped, in_sem, out_sem,
):
    blocks, width, _ = half.shape
    pairs = ((right_hbm, right_ref), (half_hbm, half), (every_hbm, every), (rot_in, rot_out))
    copies = [pltpu.make_async_copy(src, dst, in_sem.at[i]) for i, (src, dst) in enumerate(pairs)]
    for copy in copies:
        copy.start()
    for copy in copies[:3]:
        copy.wait()

    for b in range(blocks):
        result[b * width : (b + 1) * width, :width] = dot_nt(half[b], every[right_ref[b]])

    step = width // 4
    outs = []
    for part in range(4):
        for k in range(part * step, (part + 1) * step):
            flipped[k] = result[pl.ds(k, blocks, stride=width), :][:, :width].T
        rows = pl.ds(part * step, step)
        outs.append(pltpu.make_async_copy(flipped.at[rows], out_hbm.at[rows], out_sem.at[part]))
        outs[-1].start()
    for copy in outs + copies[3:]:
        copy.wait()


def shards(n_sec, n_term, wavefunction, sketch, kept, left_ids, right_ids, operators):
    sectors, m, right = wavefunction.shape
    width = sketch.shape[2]
    blocks = operators.shape[0]
    n_deep = n_sec // 4
    n_sends = (n_deep - 1) + 2 + 2 * (n_deep - 1) + n_deep
    hbm = pl.BlockSpec(memory_space=pl.ANY)
    dma = pltpu.SemaphoreType.DMA
    rotation, half, every = pl.pallas_call(
        functools.partial(kernel, n_sec, n_term),
        out_shape=(
            jax.ShapeDtypeStruct((sectors, width, m), jnp.bfloat16),
            jax.ShapeDtypeStruct((blocks, width, m), jnp.bfloat16),
            jax.ShapeDtypeStruct((n_sec * sectors, width, m), jnp.bfloat16),
        ),
        in_specs=[hbm] * 5,
        out_specs=(hbm, hbm, hbm),
        scratch_shapes=[
            pltpu.SMEM((sectors,), jnp.int32),
            pltpu.SMEM((blocks,), jnp.int32),
            pltpu.SemaphoreType.DMA((2,)),
            pltpu.SemaphoreType.DMA((n_sec + 2,)),
            pltpu.VMEM((sectors, m, right), jnp.bfloat16),
            pltpu.VMEM((sectors, width, m), F32),
            pltpu.VMEM((blocks, m, m), jnp.bfloat16),
            pltpu.VMEM((n_term, sectors, width, m), F32),
            pltpu.VMEM((sectors, width, m), jnp.bfloat16),
            pltpu.VMEM((n_sec * sectors, width, m), jnp.bfloat16),
            pltpu.VMEM((blocks, width, m), jnp.bfloat16),
            dma((sectors,)),
            dma,
            dma,
            dma((max(n_term - 1, 1), sectors)),
            dma((n_term, sectors)),
            dma((n_sends,)),
            dma((n_sec,)),
        ],
        compiler_params=pltpu.CompilerParams(
            collective_id=0, has_side_effects=True, vmem_limit_bytes=62 * 1024 * 1024
        ),
    )(kept, left_ids, wavefunction, jnp.swapaxes(sketch, 1, 2), operators)
    rotation, result = pl.pallas_call(
        right_kernel,
        out_shape=(
            jax.ShapeDtypeStruct((sectors, width, m), jnp.bfloat16),
            jax.ShapeDtypeStruct((width, width, blocks), F32),
        ),
        in_specs=[hbm] * 4,
        out_specs=(hbm, hbm),
        scratch_shapes=[
            pltpu.SMEM((blocks,), jnp.int32),
            pltpu.VMEM((blocks, width, m), jnp.bfloat16),
            pltpu.VMEM((n_sec * sectors, width, m), jnp.bfloat16),
            pltpu.VMEM((blocks * width, 128), F32),
            pltpu.VMEM((width, width, blocks), F32),
            dma((4,)),
            dma((4,)),
        ],
        compiler_params=pltpu.CompilerParams(vmem_limit_bytes=62 * 1024 * 1024),
    )(right_ids, rotation, half, every)
    return jnp.swapaxes(rotation, 1, 2), jnp.transpose(result, (2, 0, 1))


def solution(mesh):
    in_specs = (
        P("sec", None, "term"),
        P("sec", None, None),
        P("sec"),
        P(("sec", "term")),
        P(("sec", "term")),
        P(("sec", "term"), None, None),
    )
    out_specs = (P("sec", None, None), P(("sec", "term"), None, None))
    run = functools.partial(shards, mesh.shape["sec"], mesh.shape["term"])
    return jax.shard_map(run, mesh=mesh, in_specs=in_specs, out_specs=out_specs, check_vma=False)
```

```python
import functools

import jax
import jax.numpy as jnp
from jax import lax
from jax.experimental import pallas as pl
from jax.experimental.pallas import tpu as pltpu
from jax.sharding import PartitionSpec as P

HIGH = lax.Precision.HIGHEST
MESH = pl.DeviceIdType.MESH
F32 = jnp.float32


def dot_nt(a, b, precision=None):
    return lax.dot_general(
        a, b, (((1,), (1,)), ((), ())), precision=precision, preferred_element_type=F32
    )


def inverse_factors(gram, width):
    row = lax.broadcasted_iota(jnp.int32, gram.shape, 0)
    lane = lax.broadcasted_iota(jnp.int32, gram.shape, 1)
    first = lane // width * width
    eye = jnp.where(lane - first == row, 1.0, 0.0).astype(F32)
    scale = jnp.zeros_like(gram)
    for j in range(width):
        column = jnp.take_along_axis(gram, first + j, axis=1, mode="promise_in_bounds")
        root = lax.rsqrt(column[j : j + 1, :])
        scale = jnp.where(row == j, root, scale)
        if j + 1 < width:
            factor = jnp.where(row > j, column * root, 0.0)
            gram = gram - factor * (gram[j : j + 1, :] * root)
            eye = eye - factor * (eye[j : j + 1, :] * root)
    return eye * scale


def kernel(
    n_sec, n_term, kept_hbm, left_hbm, wave_hbm, sketch_hbm, ops_hbm,
    rot_out, half_out, every_out,
    kept_ref, left_ref, ids_sem, out_sem, wave, sketch, ops, part, rt, every, half,
    wave_sem, sketch_sem, ops_sem, part_send, part_recv, send_sem, recv_sem,
):
    sectors, m, _ = wave.shape
    width = sketch.shape[1]
    blocks = ops.shape[0]
    sec = lax.axis_index("sec")
    term = lax.axis_index("term")
    core = lax.rem(sec, 2)
    side = lax.rem(sec // 2, 2)
    deep = sec // 4
    n_deep = n_sec // 4

    def place(a, b, c):
        return (a * 2 + b) * 2 + c

    terms = [lax.rem(term + t, n_term) for t in range(1, n_term)]
    deeps = [lax.rem(deep + t, n_deep) for t in range(1, n_deep)]
    side_peer = place(deep, 1 - side, core)
    core_peer = place(deep, side, 1 - core)

    waves = []
    for s in range(sectors):
        waves.append(pltpu.make_async_copy(wave_hbm.at[s], wave.at[s], wave_sem.at[s]))
        waves[-1].start()
    get_sketch = pltpu.make_async_copy(sketch_hbm, sketch, sketch_sem)
    get_sketch.start()
    get_ops = pltpu.make_async_copy(ops_hbm, ops, ops_sem)
    get_ops.start()
    get_ids = []
    for i, (src, dst) in enumerate(((kept_hbm, kept_ref), (left_hbm, left_ref))):
        get_ids.append(pltpu.make_async_copy(src, dst, ids_sem.at[i]))
        get_ids[-1].start()

    barrier = pltpu.get_barrier_semaphore()
    for other in terms:
        pl.semaphore_signal(barrier, inc=1, device_id=(sec, other), device_id_type=MESH)
    peers = [place(a, side, core) for a in deeps] + [side_peer, core_peer]
    for other in peers:
        pl.semaphore_signal(barrier, inc=1, device_id=(other, term), device_id_type=MESH)

    get_sketch.wait()
    part_copies = []
    for s in range(sectors):
        waves[s].wait()
        w = wave[s]
        density = dot_nt(w, w)
        part[term, s] = jnp.dot(sketch[s], density, precision=HIGH, preferred_element_type=F32)
        if s == 0:
            pl.semaphore_wait(barrier, len(terms) + len(peers))
        for t, other in enumerate(terms):
            copy = pltpu.make_async_remote_copy(
                src_ref=part.at[term, s],
                dst_ref=part.at[term, s],
                send_sem=part_send.at[t, s],
                recv_sem=part_recv.at[term, s],
                device_id=(sec, other),
                device_id_type=MESH,
            )
            copy.start()
            part_copies.append(copy)
    for s in range(sectors):
        for other in terms:
            pltpu.make_async_remote_copy(
                src_ref=part.at[other, s],
                dst_ref=part.at[other, s],
                send_sem=part_send.at[0, s],
                recv_sem=part_recv.at[other, s],
                device_id=(sec, other),
                device_id_type=MESH,
            ).wait_recv()
    for copy in get_ids:
        copy.wait()
    total = part[0]
    for t in range(1, n_term):
        total = total + part[t]
    total = total.reshape(sectors * width, m)

    full = dot_nt(total, total, HIGH)
    owner = lax.broadcasted_iota(jnp.int32, (width, sectors * width), 1) // width
    gram = full[:width]
    for s in range(1, sectors):
        gram = jnp.where(owner == s, full[s * width : (s + 1) * width], gram)
    inverse = inverse_factors(gram, width)
    spread = jnp.concatenate([jnp.where(owner == s, inverse, 0.0) for s in range(sectors)], axis=0)
    basis = jnp.dot(spread, total, precision=HIGH, preferred_element_type=F32)
    basis = basis.reshape(sectors, width, m)
    row = lax.broadcasted_iota(jnp.int32, (width, m), 0)
    for s in range(sectors):
        kept_rows = jnp.where(row < kept_ref[s], basis[s], 0.0).astype(jnp.bfloat16)
        rt[s] = kept_rows
        every[sec * sectors + s] = kept_rows

    sends = []

    def send(src, slot, device):
        copy = pltpu.make_async_remote_copy(
            src_ref=src,
            dst_ref=every.at[pl.ds(slot * sectors, sectors)],
            send_sem=send_sem.at[len(sends)],
            recv_sem=recv_sem.at[slot],
            device_id=(device, term),
            device_id_type=MESH,
        )
        copy.start()
        sends.append(copy)

    def keep(slot):
        rows = pl.ds(slot * sectors, sectors)
        outs.append(pltpu.make_async_copy(every.at[rows], every_out.at[rows], out_sem.at[len(outs)]))
        outs[-1].start()

    def arrived(slot):
        part_of = every.at[pl.ds(slot * sectors, sectors)]
        pltpu.make_async_remote_copy(
            src_ref=part_of,
            dst_ref=part_of,
            send_sem=send_sem.at[0],
            recv_sem=recv_sem.at[slot],
            device_id=(core_peer, term),
            device_id_type=MESH,
        ).wait_recv()
        keep(slot)
        return part_of

    for a in deeps:
        send(rt, sec, place(a, side, core))
    send(rt, sec, side_peer)
    send(rt, sec, core_peer)

    outs = [pltpu.make_async_copy(rt, rot_out, out_sem.at[0])]
    outs[0].start()
    keep(sec)
    get_ops.wait()

    def left_side(start, stop):
        @pl.loop(start, stop, step=8)
        def _(first):
            for i in range(8):
                b = first + i
                rotated = jnp.dot(rt[lax.rem(left_ref[b], sectors)], ops[b], preferred_element_type=F32)
                half[b] = rotated.astype(jnp.bfloat16)

    left_side(0, blocks // 4)
    for a in deeps:
        slot = place(a, side, core)
        block = arrived(slot)
        send(block, slot, side_peer)
    for a in deeps:
        slot = place(a, side, core)
        send(every.at[pl.ds(slot * sectors, sectors)], slot, core_peer)
    left_side(blocks // 4, blocks)
    outs.append(pltpu.make_async_copy(half, half_out, out_sem.at[len(outs)]))
    outs[-1].start()
    for a in [deep] + deeps:
        slot = place(a, 1 - side, core)
        block = arrived(slot)
        send(block, slot, core_peer)
    for a in [deep] + deeps:
        for b in range(2):
            arrived(place(a, b, 1 - core))

    for copy in outs:
        copy.wait()
    for copy in part_copies + sends:
        copy.wait_send()


def right_kernel(
    right_hbm, rot_in, half_hbm, every_hbm, rot_out, out_hbm,
    right_ref, half, every, result, flipped, in_sem, out_sem,
):
    blocks, width, _ = half.shape
    pairs = ((right_hbm, right_ref), (half_hbm, half), (every_hbm, every), (rot_in, rot_out))
    copies = [pltpu.make_async_copy(src, dst, in_sem.at[i]) for i, (src, dst) in enumerate(pairs)]
    for copy in copies:
        copy.start()
    for copy in copies[:3]:
        copy.wait()

    for b in range(blocks):
        result[b * width : (b + 1) * width, :width] = dot_nt(half[b], every[right_ref[b]])

    step = width // 4
    outs = []
    for part in range(4):
        for k in range(part * step, (part + 1) * step):
            flipped[k] = result[pl.ds(k, blocks, stride=width), :][:, :width].T
        rows = pl.ds(part * step, step)
        outs.append(pltpu.make_async_copy(flipped.at[rows], out_hbm.at[rows], out_sem.at[part]))
        outs[-1].start()
    for copy in outs + copies[3:]:
        copy.wait()


def shards(n_sec, n_term, wavefunction, sketch, kept, left_ids, right_ids, operators):
    sectors, m, right = wavefunction.shape
    width = sketch.shape[2]
    blocks = operators.shape[0]
    n_deep = n_sec // 4
    n_sends = (n_deep - 1) + 2 + 2 * (n_deep - 1) + n_deep
    hbm = pl.BlockSpec(memory_space=pl.ANY)
    dma = pltpu.SemaphoreType.DMA
    rotation, half, every = pl.pallas_call(
        functools.partial(kernel, n_sec, n_term),
        out_shape=(
            jax.ShapeDtypeStruct((sectors, width, m), jnp.bfloat16),
            jax.ShapeDtypeStruct((blocks, width, m), jnp.bfloat16),
            jax.ShapeDtypeStruct((n_sec * sectors, width, m), jnp.bfloat16),
        ),
        in_specs=[hbm] * 5,
        out_specs=(hbm, hbm, hbm),
        scratch_shapes=[
            pltpu.SMEM((sectors,), jnp.int32),
            pltpu.SMEM((blocks,), jnp.int32),
            pltpu.SemaphoreType.DMA((2,)),
            pltpu.SemaphoreType.DMA((n_sec + 2,)),
            pltpu.VMEM((sectors, m, right), jnp.bfloat16),
            pltpu.VMEM((sectors, width, m), F32),
            pltpu.VMEM((blocks, m, m), jnp.bfloat16),
            pltpu.VMEM((n_term, sectors, width, m), F32),
            pltpu.VMEM((sectors, width, m), jnp.bfloat16),
            pltpu.VMEM((n_sec * sectors, width, m), jnp.bfloat16),
            pltpu.VMEM((blocks, width, m), jnp.bfloat16),
            dma((sectors,)),
            dma,
            dma,
            dma((max(n_term - 1, 1), sectors)),
            dma((n_term, sectors)),
            dma((n_sends,)),
            dma((n_sec,)),
        ],
        compiler_params=pltpu.CompilerParams(
            collective_id=0, has_side_effects=True, vmem_limit_bytes=62 * 1024 * 1024
        ),
    )(kept, left_ids, wavefunction, jnp.swapaxes(sketch, 1, 2), operators)
    rotation, result = pl.pallas_call(
        right_kernel,
        out_shape=(
            jax.ShapeDtypeStruct((sectors, width, m), jnp.bfloat16),
            jax.ShapeDtypeStruct((width, width, blocks), F32),
        ),
        in_specs=[hbm] * 4,
        out_specs=(hbm, hbm),
        scratch_shapes=[
            pltpu.SMEM((blocks,), jnp.int32),
            pltpu.VMEM((blocks, width, m), jnp.bfloat16),
            pltpu.VMEM((n_sec * sectors, width, m), jnp.bfloat16),
            pltpu.VMEM((blocks * width, 128), F32),
            pltpu.VMEM((width, width, blocks), F32),
            dma((4,)),
            dma((4,)),
        ],
        compiler_params=pltpu.CompilerParams(vmem_limit_bytes=62 * 1024 * 1024),
    )(right_ids, rotation, half, every)
    return jnp.swapaxes(rotation, 1, 2), jnp.transpose(result, (2, 0, 1))


def solution(mesh):
    in_specs = (
        P("sec", None, "term"),
        P("sec", None, None),
        P("sec"),
        P(("sec", "term")),
        P(("sec", "term")),
        P(("sec", "term"), None, None),
    )
    out_specs = (P("sec", None, None), P(("sec", "term"), None, None))
    run = functools.partial(shards, mesh.shape["sec"], mesh.shape["term"])
    return jax.shard_map(run, mesh=mesh, in_specs=in_specs, out_specs=out_specs, check_vma=False)
```
